256 devices in a mesh: segment: 16 (over x_lo, z), tp: 16 (over y, x_hi, core).
Axes of the slice: x: 4 (x_hi: 2, x_lo: 2; x = x_hi * 2 + x_lo), y: 4, z: 8, core: 2. Of those that a mesh axis runs over, the one named last changes fastest.
Arguments:
- layer_inputs: bfloat16 [16, 2, 128, 2048], P('segment', None, 'tp'), may hold values from -100 to 100, as said below
- cotangent: bfloat16 [2, 2, 128, 2048], P(None, None, 'tp'), may hold values from -6 to 6
- gate_weight: bfloat16 [16, 2048, 4096], P('segment', None, 'tp'), may hold values from -1 to 1, as said below
- up_weight: bfloat16 [16, 2048, 4096], P('segment', None, 'tp'), may hold values from -1 to 1, as said below
- down_weight: bfloat16 [16, 4096, 2048], P('segment', 'tp'), may hold values from -1 to 1, as said below
- gate_momentum: float32 [16, 1024, 4096], P('segment', None, 'tp'), may hold values from -48 to 48
- up_momentum: float32 [16, 1024, 4096], P('segment', None, 'tp'), may hold values from -48 to 48
- down_momentum: float32 [16, 4096, 1024], P('segment', 'tp'), may hold values from -48 to 48
Outputs:
- input_gradient: bfloat16 [16, 2, 128, 2048], P('segment', None, 'tp')
- new_gate_momentum: float32 [16, 1024, 4096], P('segment', None, 'tp')
- new_up_momentum: float32 [16, 1024, 4096], P('segment', None, 'tp')
- new_down_momentum: float32 [16, 4096, 1024], P('segment', 'tp')
The draws below stay inside these ranges and needn't reach their ends.
Inputs may be any that keep to these rules, and one draw needn't show every extreme that they name: `layer_inputs`: stored layer inputs, independent for every section and micro-batch. `gate_weight`: sections 2l and 2l + 1 hold equal copies of one layer's weights. `up_weight`: sections 2l and 2l + 1 hold equal copies of one layer's weights. `down_weight`: sections 2l and 2l + 1 hold equal copies of one layer's weights.
All inputs are finite; a program needn't handle non-finite values.
Results may differ from the reference program's by a relative error of at most 0.02.
Values may be sent and summed in bfloat16 or wider, within the bound.
No kernel may reach another device: no remote copies, remote signals or barrier semaphores. Data moves between devices by JAX's collectives and lax.ppermute only.
A program may use at most 64 MiB of HBM per device.

```python
import math
import jax
import jax.numpy as jnp
from jax import lax

D = 2048
FF = 4096
ROWS = 128
MICRO = 2
LAYERS = 8
HALF = 1024
FF_DEV = 256
N_TP = 16


def clipped_normal(key, shape):
    return jnp.clip(jax.random.normal(key, shape, jnp.float32), -4.0, 4.0)


def draw_layer_inputs(key, part):
    shape = (2 * LAYERS, MICRO, ROWS, D)
    noise_key, row_key, column_key = jax.random.split(jax.random.fold_in(key, 101), 3)
    noise = clipped_normal(noise_key, shape)
    row_scale = jnp.exp(jax.random.uniform(row_key, (2 * LAYERS, MICRO, ROWS, 1), jnp.float32, 0.0, math.log(10.0)))
    column_scale = jnp.exp(jax.random.uniform(column_key, (2 * LAYERS, MICRO, 1, D), jnp.float32, math.log(0.25), math.log(2.5)))
    return (noise * row_scale * column_scale).astype(jnp.bfloat16)


def mirrored(key, shape, fan_in):
    values = clipped_normal(key, shape)
    values = values * fan_in ** (-0.5)
    return jnp.repeat(values, 2, axis=0).astype(jnp.bfloat16)


def draw_gate_weight(key, part):
    return mirrored(jax.random.fold_in(key, 211), (LAYERS, D, FF), D)


def draw_up_weight(key, part):
    return mirrored(jax.random.fold_in(key, 223), (LAYERS, D, FF), D)


def draw_down_weight(key, part):
    return mirrored(jax.random.fold_in(key, 227), (LAYERS, FF, D), FF)


def block_levels(key, extent, cuts, low, largest):
    def one(dim, shards_of):
        steps = jax.random.uniform(jax.random.fold_in(jax.random.fold_in(key, 6), dim), (shards_of,), jnp.float32, low / len(cuts), largest / len(cuts))
        return jnp.repeat(jnp.exp(steps), extent[dim] // shards_of).reshape((-1,) + (1,) * (len(extent) - dim - 1))

    loudness = one(*cuts[0])
    for cut in cuts[1:]:
        loudness = loudness * one(*cut)
    return loudness


def centred(stream_key, extent, deviation, most, cuts=(), held_as=jnp.bfloat16):
    entries = deviation * jax.random.normal(stream_key, extent, jnp.float32)
    if cuts:
        entries = entries * block_levels(stream_key, extent, cuts, -0.22, 0.18)
    return jnp.clip(entries, -most, most).astype(held_as)


def setup_inputs(seed: int = 0) -> dict:
    key_list = jax.random.split(jax.random.key(seed), 9)
    layer_inputs = draw_layer_inputs(jax.random.fold_in(key_list[8], 71), 0)
    cotangent = centred(key_list[1], (2, MICRO, ROWS, D), 1.0, 6.0, ((2, 16),))
    gate_weight = draw_gate_weight(jax.random.fold_in(key_list[8], 71), 0)
    up_weight = draw_up_weight(jax.random.fold_in(key_list[8], 71), 0)
    down_weight = draw_down_weight(jax.random.fold_in(key_list[8], 71), 0)
    gate_momentum = centred(key_list[5], (2 * LAYERS, HALF, FF), 8.0, 48.0, ((0, 16), (2, 16)), jnp.float32)
    up_momentum = centred(key_list[6], (2 * LAYERS, HALF, FF), 8.0, 48.0, ((0, 16), (2, 16)), jnp.float32)
    down_momentum = centred(key_list[7], (2 * LAYERS, FF, HALF), 8.0, 48.0, ((0, 16), (1, 16)), jnp.float32)
    return dict(layer_inputs=layer_inputs, cotangent=cotangent, gate_weight=gate_weight, up_weight=up_weight, down_weight=down_weight, gate_momentum=gate_momentum, up_momentum=up_momentum, down_momentum=down_momentum)


epsilon = 1e-05
momentum_decay = 0.9

def rounded(values):
    return lax.optimization_barrier(values.astype(jnp.bfloat16)).astype(jnp.float32)

def section_backward(inputs, incoming, gate_weight, up_weight, down_weight):
    rows = inputs.reshape(-1, D).astype(jnp.float32)
    inverse_norm = lax.rsqrt(lax.optimization_barrier(jnp.mean(rows * rows, axis=-1, keepdims=True)) + epsilon)
    exact = rows * inverse_norm
    normed = exact.astype(jnp.bfloat16)
    gate = jnp.dot(normed, gate_weight, preferred_element_type=jnp.float32)
    up = jnp.dot(normed, up_weight, preferred_element_type=jnp.float32)
    sigma = jax.nn.sigmoid(gate)
    silu = gate * sigma
    hidden = (silu * up).astype(jnp.bfloat16)
    arriving = incoming.reshape(-1, D)
    hidden_grad = jnp.dot(arriving, down_weight.T, preferred_element_type=jnp.float32)
    gate_grad = (hidden_grad * up * sigma * (1.0 + gate * (1.0 - sigma))).astype(jnp.bfloat16)
    up_grad = (hidden_grad * silu).astype(jnp.bfloat16)
    gate_parts = jnp.einsum('rgf,dgf->grd', gate_grad.astype(jnp.float32).reshape(-1, N_TP, FF_DEV), gate_weight.astype(jnp.float32).reshape(D, N_TP, FF_DEV), precision=lax.Precision.HIGHEST)
    up_parts = jnp.einsum('rgf,dgf->grd', up_grad.astype(jnp.float32).reshape(-1, N_TP, FF_DEV), up_weight.astype(jnp.float32).reshape(D, N_TP, FF_DEV), precision=lax.Precision.HIGHEST)
    parts = lax.optimization_barrier((gate_parts + up_parts).astype(jnp.bfloat16))
    normed_grad = lax.optimization_barrier(jnp.sum(parts.astype(jnp.float32), axis=0))
    back = arriving.astype(jnp.float32) + inverse_norm * (normed_grad - exact * lax.optimization_barrier(jnp.mean(normed_grad * exact, axis=-1, keepdims=True)))
    back = back.astype(jnp.bfloat16).reshape(inputs.shape)
    weights = (jnp.dot(normed.T, gate_grad, preferred_element_type=jnp.float32), jnp.dot(normed.T, up_grad, preferred_element_type=jnp.float32), jnp.dot(hidden.T, arriving, preferred_element_type=jnp.float32))
    return (back, weights)

def reference(layer_inputs, cotangent, gate_weight, up_weight, down_weight, gate_momentum, up_momentum, down_momentum):

    def step(incoming, position):
        sections = (2 * position, 2 * position + 1)
        backs = []
        totals = []
        for direction in range(2):
            section = sections[direction]
            back, weights = section_backward(lax.dynamic_index_in_dim(layer_inputs, section, 0, False), incoming[direction], lax.dynamic_index_in_dim(gate_weight, section, 0, False), lax.dynamic_index_in_dim(up_weight, section, 0, False), lax.dynamic_index_in_dim(down_weight, section, 0, False))
            backs.append(back)
            totals.append(weights)
        lower_sum = [totals[0][which] + rounded(totals[1][which]) for which in range(3)]
        upper_sum = [totals[1][which] + rounded(totals[0][which]) for which in range(3)]
        lower = (momentum_decay * gate_momentum[sections[0]] + lower_sum[0][:HALF], momentum_decay * up_momentum[sections[0]] + lower_sum[1][:HALF], momentum_decay * down_momentum[sections[0]] + lower_sum[2][:, :HALF])
        upper = (momentum_decay * gate_momentum[sections[1]] + upper_sum[0][HALF:], momentum_decay * up_momentum[sections[1]] + upper_sum[1][HALF:], momentum_decay * down_momentum[sections[1]] + upper_sum[2][:, HALF:])
        stacked = jnp.stack(backs)
        return (stacked, (stacked, lower, upper))
    positions = jnp.arange(LAYERS, dtype=jnp.int32)
    _, (backs, lower, upper) = lax.scan(step, cotangent, positions)
    input_gradient = backs.reshape((2 * LAYERS,) + backs.shape[2:])
    results = []
    for which in range(3):
        paired = jnp.stack([lower[which], upper[which]], axis=1)
        results.append(paired.reshape((2 * LAYERS,) + paired.shape[2:]))
    return (input_gradient, results[0], results[1], results[2])
```

```python
import jax
import jax.numpy as jnp
from jax import lax
from jax.sharding import PartitionSpec as P

epsilon = 1e-05
momentum_decay = 0.9
bf16 = jnp.bfloat16
f32 = jnp.float32


def dot(left, right, dims):
    return lax.dot_general(left, right, ((dims[:1], dims[1:]), ((), ())), preferred_element_type=f32)


def shards(
    layer_inputs,
    cotangent,
    gate_weight,
    up_weight,
    down_weight,
    gate_momentum,
    up_momentum,
    down_momentum,
):
    segments = lax.axis_size("segment")
    tp = lax.axis_size("tp")
    depth = segments // 2
    segment = lax.axis_index("segment")
    direction = segment % 2
    position = segment // 2
    core = lax.axis_index("tp") % 2
    width = layer_inputs.shape[3]
    half = width // 2
    hidden_dev = gate_weight.shape[2]
    chips = [list(range(c, tp, 2)) for c in range(2)]
    other_core = [(i, i ^ 1) for i in range(tp)]
    pair = [(i, i ^ 1) for i in range(segments)]
    mirror = [
        ((s * tp + t), ((s ^ 1) * tp + (t ^ 1))) for s in range(segments) for t in range(tp)
    ]

    def swap(block):
        return lax.ppermute(block, "tp", other_core)

    def gathered(rows):
        copies = jnp.broadcast_to(rows[None], (tp // 2,) + rows.shape)
        out = lax.all_to_all(copies, "tp", 0, 0, axis_index_groups=chips, tiled=True)
        return out

    def scattered(parts):
        blocks = parts.reshape(tp // 2, -1, width)
        out = lax.all_to_all(blocks, "tp", 0, 0, axis_index_groups=chips, tiled=True)
        return jnp.sum(out.astype(f32), axis=0)

    entry = lax.dynamic_index_in_dim(cotangent, direction, 0, keepdims=False)
    stacked = jnp.stack([layer_inputs[0], entry], axis=1)
    mine = lax.dynamic_index_in_dim(stacked, core, 0, keepdims=False)
    theirs = lax.dynamic_index_in_dim(stacked, 1 - core, 0, keepdims=False)
    block = jnp.concatenate([mine, swap(theirs)], axis=1)
    inputs = block[0].astype(f32)
    rows_chip = inputs.shape[0]
    inverse_norm = lax.rsqrt(jnp.mean(inputs * inputs, axis=-1, keepdims=True) + epsilon)
    exact = inputs * inverse_norm
    normed = exact.astype(bf16)
    local_in = block[1]

    gate_w = jnp.concatenate([gate_weight[0], swap(gate_weight[0])], axis=1)
    up_w = jnp.concatenate([up_weight[0], swap(up_weight[0])], axis=1)
    down_w = jnp.concatenate([down_weight[0], swap(down_weight[0])], axis=0)

    first = gathered(jnp.concatenate([normed, local_in], axis=0))
    full_normed = first[:, :rows_chip].reshape(-1, width)
    full_in = first[:, rows_chip:].reshape(-1, width)

    gate = dot(full_normed, gate_w, (1, 0))
    up = dot(full_normed, up_w, (1, 0))
    sigma = jax.nn.sigmoid(gate)
    silu = gate * sigma
    hidden = (silu * up).astype(bf16)
    slope = up * sigma * (1.0 + gate * (1.0 - sigma))

    for tick in range(depth):
        if tick:
            route = [(2 * tick - 2 + d, 2 * tick + d) for d in range(2)]
            received = lax.ppermute(back, "segment", route)
            local_in = jnp.where(position == tick, received, local_in)
            full_in = gathered(local_in).reshape(-1, width)
        hidden_grad = dot(full_in, down_w, (1, 1))
        gate_grad = (hidden_grad * slope).astype(bf16)
        up_grad = (hidden_grad * silu).astype(bf16)
        parts = dot(gate_grad, gate_w, (1, 1)) + dot(up_grad, up_w, (1, 1))
        normed_grad = scattered(parts.astype(bf16))
        back = local_in.astype(f32) + inverse_norm * (
            normed_grad - exact * jnp.mean(normed_grad * exact, axis=-1, keepdims=True)
        )
        back = back.astype(bf16)

    rows_dev = rows_chip // 2
    mine_back, other_back = back[:rows_dev], swap(back[rows_dev:])
    low = core == 0
    input_gradient = jnp.stack(
        [jnp.where(low, mine_back, other_back), jnp.where(low, other_back, mine_back)]
    )

    keep = direction * half
    give = half - keep

    def features(rows, start):
        return lax.dynamic_slice_in_dim(rows, start, half, 1)

    def all_rows(rows):
        here = jnp.concatenate(
            [features(rows, keep), lax.ppermute(features(rows, give), "segment", pair)], axis=0
        )
        return jnp.concatenate([here, swap(here)], axis=0)

    def all_units(units):
        own, other = units[:, :hidden_dev], units[:, hidden_dev:]
        return jnp.concatenate(
            [
                own,
                lax.ppermute(own, "segment", pair),
                swap(other),
                lax.ppermute(other, ("segment", "tp"), mirror),
            ],
            axis=0,
        )

    def of(units, which):
        return lax.slice_in_dim(units, which * hidden_dev, (which + 1) * hidden_dev, axis=1)

    factors = [
        jnp.concatenate([of(hidden, w), of(gate_grad, w), of(up_grad, w)], axis=1) for w in range(2)
    ]
    units = jnp.concatenate(
        [
            factors[0],
            lax.ppermute(factors[0], "segment", pair),
            swap(factors[1]),
            lax.ppermute(factors[1], ("segment", "tp"), mirror),
        ],
        axis=0,
    )
    rows_normed = all_rows(full_normed)
    rows_in = all_rows(full_in)
    gate_share = dot(rows_normed, of(units, 1), (0, 0))
    up_share = dot(rows_normed, of(units, 2), (0, 0))
    down_share = dot(of(units, 0), rows_in, (0, 0))
    new_gate = (momentum_decay * gate_momentum[0] + gate_share)[None]
    new_up = (momentum_decay * up_momentum[0] + up_share)[None]
    new_down = (momentum_decay * down_momentum[0] + down_share)[None]
    return (input_gradient[None], new_gate, new_up, new_down)


def solution(mesh):
    return jax.shard_map(
        shards,
        mesh=mesh,
        in_specs=(
            P("segment", None, "tp", None),
            P(None, None, "tp", None),
            P("segment", None, "tp"),
            P("segment", None, "tp"),
            P("segment", "tp", None),
            P("segment", None, "tp"),
            P("segment", None, "tp"),
            P("segment", "tp", None),
        ),
        out_specs=(
            P("segment", None, "tp", None),
            P("segment", None, "tp"),
            P("segment", None, "tp"),
            P("segment", "tp", None),
        ),
        check_vma=False,
    )
```

```python
import functools

import jax
import jax.numpy as jnp
from jax import lax
from jax.experimental import pallas as pl
from jax.experimental.pallas import tpu as pltpu
from jax.sharding import PartitionSpec as P

epsilon = 1e-05
momentum_decay = 0.9
bf16 = jnp.bfloat16
f32 = jnp.float32


def dot(left, right, dims):
    return lax.dot_general(left, right, ((dims[:1], dims[1:]), ((), ())), preferred_element_type=f32)


def tick_kernel(ways, chunk, keep_units, *refs):
    sources, refs = refs[:ways], refs[ways:]
    own, rest, refs = refs[:3], refs[3:8], refs[8:]
    outs, rows_ref = refs[:-1], refs[-1]
    each, width = sources[0].shape
    units = own[0].shape[0]
    silu, slope, down, gate, up = rest
    for w in range(ways):
        rows_ref[w * each : (w + 1) * each, :] = sources[w][...]
    gate_grads, up_grads = [], []
    for b, weight in enumerate((own[0], down)):
        hidden_grad = dot(rows_ref[...], weight[...], (1, 1))
        span = slice(b * units, (b + 1) * units)
        gate_grads.append((hidden_grad * slope[:, span]).astype(bf16))
        up_grads.append((hidden_grad * silu[:, span]).astype(bf16))
        if keep_units:
            outs[ways][:, span] = gate_grads[-1]
            outs[ways + 1][:, span] = up_grads[-1]
    for c in range(width // chunk):
        rows = slice(c * chunk, (c + 1) * chunk)
        total = dot(gate_grads[0], own[1][rows, :], (1, 1))
        total = total + dot(up_grads[0], own[2][rows, :], (1, 1))
        total = total + dot(gate_grads[1], gate[rows, :], (1, 1))
        total = total + dot(up_grads[1], up[rows, :], (1, 1))
        total = total.astype(bf16)
        for w in range(ways):
            outs[w][:, rows] = total[w * each : (w + 1) * each]


def tick_parts(sources, own, rest, keep_units):
    ways = len(sources)
    each, width = sources[0].shape
    count = ways * each
    units = own[0].shape[0]
    chunk = 512
    out_shape = [jax.ShapeDtypeStruct((each, width), bf16)] * ways
    aliases = {}
    if keep_units:
        out_shape += [jax.ShapeDtypeStruct((count, 2 * units), bf16)] * 2
    inside = pl.BlockSpec(memory_space=pltpu.VMEM)
    results = pl.pallas_call(
        lambda *refs: tick_kernel(ways, chunk, keep_units, *refs),
        out_shape=out_shape,
        in_specs=[inside] * (ways + 3 + len(rest)),
        out_specs=[inside] * len(out_shape),
        scratch_shapes=[pltpu.VMEM((count, width), bf16)],
        input_output_aliases=aliases,
        compiler_params=pltpu.CompilerParams(vmem_limit_bytes=8 * 1024 * 1024),
        cost_estimate=pl.CostEstimate(
            flops=12 * count * width * units, bytes_accessed=12 * width * units, transcendentals=0
        ),
    )(*sources, *own, *rest)
    return results[:ways], results[ways:] if keep_units else rest


def share_kernel(*refs):
    pieces, (local_ref, inputs_ref, norm_ref, out_ref) = refs[:-4], refs[-4:]
    total = pieces[0][...].astype(f32)
    for piece in pieces[1:]:
        total = total + piece[...].astype(f32)
    scale = norm_ref[...]
    exact = inputs_ref[...].astype(f32) * scale
    centre = jnp.mean(total * exact, axis=-1, keepdims=True)
    share = 0.5 * local_ref[...].astype(f32) + scale * (total - exact * centre)
    out_ref[...] = share.astype(bf16)


def advance_kernel(tick, turn_ref, straight_ref, crossed_ref, local_ref, out_ref):
    received = (straight_ref[...].astype(f32) + crossed_ref[...].astype(f32)).astype(bf16)
    out_ref[...] = jnp.where(turn_ref[0] == tick, received, local_ref[...])


def small_call(kernel, like, *operands, scalar=False):
    inside = pl.BlockSpec(memory_space=pltpu.VMEM)
    specs = [inside] * len(operands)
    if scalar:
        specs[0] = pl.BlockSpec(memory_space=pltpu.SMEM)
    return pl.pallas_call(
        kernel,
        out_shape=jax.ShapeDtypeStruct(like.shape, like.dtype),
        in_specs=specs,
        out_specs=inside,
        compiler_params=pltpu.CompilerParams(vmem_limit_bytes=4 * 1024 * 1024),
        cost_estimate=pl.CostEstimate(flops=8 * like.size, bytes_accessed=8 * like.size, transcendentals=0),
    )(*operands)


def shards(
    layer_inputs,
    cotangent,
    gate_weight,
    up_weight,
    down_weight,
    gate_momentum,
    up_momentum,
    down_momentum,
):
    segments = lax.axis_size("segment")
    tp = lax.axis_size("tp")
    depth = segments // 2
    segment = lax.axis_index("segment")
    direction = segment % 2
    position = segment // 2
    core = lax.axis_index("tp") % 2
    side = lax.axis_index("tp") // 2 % 2
    width = layer_inputs.shape[3]
    half = width // 2
    hidden_dev = gate_weight.shape[2]
    ways = tp // 4
    other_core = [(i, i ^ 1) for i in range(tp)]
    other_side = [(i, i ^ 2) for i in range(tp)]
    pair = [(i, i ^ 1) for i in range(segments)]
    mirror = [
        ((s * tp + t), ((s ^ 1) * tp + (t ^ 1))) for s in range(segments) for t in range(tp)
    ]

    def swap(block):
        return lax.ppermute(block, "tp", other_core)

    def along_y(block, distance):
        return lax.ppermute(block, "tp", [(i, (i + 4 * distance) % tp) for i in range(tp)])

    order = [1, ways - 1, *range(2, ways - 1)]

    def gathered(rows):
        out = {d: along_y(rows, d) for d in order}
        return [rows] + [out[d] for d in range(1, ways)]

    def scattered(parts):
        return [parts[0]] + [along_y(parts[d], ways - d) for d in order]

    def in_order(index, mine, theirs, axis):
        return jnp.where(
            index == 0,
            jnp.concatenate([mine, theirs], axis=axis),
            jnp.concatenate([theirs, mine], axis=axis),
        )

    trade = depth // 2
    part = jnp.where(position < trade, core, 1 - core)
    entry = lax.dynamic_index_in_dim(cotangent, direction, 0, keepdims=False)
    stacked = jnp.stack([layer_inputs[0], entry], axis=1)
    mine = lax.dynamic_index_in_dim(stacked, part, 0, keepdims=False)
    theirs = lax.dynamic_index_in_dim(stacked, 1 - part, 0, keepdims=False)
    block = in_order(core, mine, swap(theirs), 1)
    block = in_order(side, block, lax.ppermute(block, "tp", other_side), 1)
    inputs = block[0].astype(f32)
    rows_own = inputs.shape[0]
    inverse_norm = lax.rsqrt(jnp.mean(inputs * inputs, axis=-1, keepdims=True) + epsilon)
    exact = inputs * inverse_norm
    normed = exact.astype(bf16)
    local_in = block[1]

    gate_w = [gate_weight[0], swap(gate_weight[0])]
    up_w = [up_weight[0], swap(up_weight[0])]
    down_w = [down_weight[0], swap(down_weight[0])]

    first = gathered(jnp.concatenate([normed, local_in], axis=0))
    full_normed = jnp.concatenate([piece[:rows_own] for piece in first], axis=0)
    incoming = [piece[rows_own:] for piece in first]

    gate = jnp.concatenate([dot(full_normed, w, (1, 0)) for w in gate_w], axis=1)
    up = jnp.concatenate([dot(full_normed, w, (1, 0)) for w in up_w], axis=1)
    sigma = jax.nn.sigmoid(gate)
    silu = gate * sigma
    hidden = (silu * up).astype(bf16)
    slope = up * sigma * (1.0 + gate * (1.0 - sigma))

    keep = direction * half
    give = half - keep

    def features(rows, start):
        return lax.dynamic_slice_in_dim(rows, start, half, 1)

    def mirrored(rows):
        return lax.ppermute(rows, "segment", pair)

    def own(units):
        return units[:, :hidden_dev]

    def other(units):
        return units[:, hidden_dev:]

    def sent(units_own, units_other):
        return (
            units_own,
            mirrored(units_own),
            swap(units_other),
            lax.ppermute(units_other, ("segment", "tp"), mirror),
        )

    def placed(arrays, space):
        return [pltpu.with_memory_space_constraint(a, space) for a in arrays]

    own_w = placed([down_w[0], gate_w[0], up_w[0]], pltpu.VMEM)
    rest = placed([silu, slope, down_w[1], gate_w[1], up_w[1]], pltpu.VMEM)
    turn = position.astype(jnp.int32).reshape(1)
    stored = block[0]
    side_rows, side_hidden = mirrored(features(full_normed, give)), mirrored(hidden)
    for tick in range(depth):
        last = tick == depth - 1
        if tick:
            route = [(2 * tick - 2 + d, 2 * tick + d) for d in range(2)]
            turned = 1 if tick == trade else 0
            ahead = [(a * tp + t, b * tp + (t ^ turned)) for a, b in route for t in range(tp)]
            across = [(a * tp + t, b * tp + (t ^ turned ^ 2)) for a, b in route for t in range(tp)]
            straight = lax.ppermute(back, ("segment", "tp"), ahead)
            crossed = lax.ppermute(back, ("segment", "tp"), across)
            local_in = small_call(
                functools.partial(advance_kernel, tick), local_in, turn, straight, crossed, local_in, scalar=True
            )
            if tick == 2:
                local_in, side_rows, side_hidden = lax.optimization_barrier(
                    (local_in, side_rows, side_hidden)
                )
            incoming = gathered(local_in)
        parts, rest = tick_parts(incoming, own_w, rest, last)
        pieces = scattered(parts)
        back = small_call(share_kernel, local_in, *pieces, local_in, stored, inverse_norm)
    gate_grad, up_grad, full_normed, hidden, side_rows, side_hidden, incoming, _ = lax.optimization_barrier(
        (*rest, full_normed, hidden, side_rows, side_hidden, incoming, pieces[1])
    )
    full_in = jnp.concatenate(incoming, axis=0)

    quarter = rows_own // 4
    here = lax.dynamic_slice_in_dim(back, side * 2 * quarter, 2 * quarter, 0)
    there = lax.dynamic_slice_in_dim(back, (1 - side) * 2 * quarter, 2 * quarter, 0)
    arrived = lax.ppermute(there, "tp", other_side)
    total = (here.astype(f32) + arrived.astype(f32)).astype(bf16)
    mine_back = lax.dynamic_slice_in_dim(total, core * quarter, quarter, 0)
    other_back = swap(lax.dynamic_slice_in_dim(total, (1 - core) * quarter, quarter, 0))
    low = part == 0
    input_gradient = jnp.stack(
        [jnp.where(low, mine_back, other_back), jnp.where(low, other_back, mine_back)]
    )

    slopes = jnp.concatenate(
        sent(
            jnp.concatenate([own(gate_grad), own(up_grad)], axis=1),
            jnp.concatenate([other(gate_grad), other(up_grad)], axis=1),
        ),
        axis=0,
    )
    def from_both(here, there):
        return jnp.concatenate([here, swap(there)], axis=0)

    here = jnp.concatenate([features(full_in, keep), mirrored(features(full_in, give))], axis=0)
    rows_in = from_both(here, here)
    here = jnp.concatenate([features(full_normed, keep), side_rows], axis=0)
    rows_normed = from_both(here, here)
    here = jnp.concatenate([hidden, side_hidden], axis=0)
    rows_hidden = from_both(own(here), other(here))
    gate_share = dot(rows_normed, own(slopes), (0, 0))
    up_share = dot(rows_normed, other(slopes), (0, 0))
    down_share = dot(rows_hidden, rows_in, (0, 0))
    new_gate = (momentum_decay * gate_momentum[0] + gate_share)[None]
    new_up = (momentum_decay * up_momentum[0] + up_share)[None]
    new_down = (momentum_decay * down_momentum[0] + down_share)[None]
    return (input_gradient[None], new_gate, new_up, new_down)


def solution(mesh):
    return jax.shard_map(
        shards,
        mesh=mesh,
        in_specs=(
            P("segment", None, "tp", None),
            P(None, None, "tp", None),
            P("segment", None, "tp"),
            P("segment", None, "tp"),
            P("segment", "tp", None),
            P("segment", None, "tp"),
            P("segment", None, "tp"),
            P("segment", "tp", None),
        ),
        out_specs=(
            P("segment", None, "tp", None),
            P("segment", None, "tp"),
            P("segment", None, "tp"),
            P("segment", "tp", None),
        ),
        check_vma=False,
    )
```

```python
import functools

import jax
import jax.numpy as jnp
from jax import lax
from jax.experimental import pallas as pl
from jax.experimental.pallas import tpu as pltpu
from jax.sharding import PartitionSpec as P

epsilon = 1e-05
momentum_decay = 0.9
bf16 = jnp.bfloat16
f32 = jnp.float32


def dot(left, right, dims):
    return lax.dot_general(left, right, ((dims[:1], dims[1:]), ((), ())), preferred_element_type=f32)


def tick_kernel(ways, chunk, keep_units, *refs):
    sources, refs = refs[:ways], refs[ways:]
    own, rest, refs = refs[:3], refs[3:8], refs[8:]
    outs, rows_ref = refs[:-1], refs[-1]
    each, width = sources[0].shape
    units = own[0].shape[0]
    silu, slope, down, gate, up = rest
    for w in range(ways):
        rows_ref[w * each : (w + 1) * each, :] = sources[w][...]
    gate_grads, up_grads = [], []
    for b, weight in enumerate((own[0], down)):
        hidden_grad = dot(rows_ref[...], weight[...], (1, 1))
        span = slice(b * units, (b + 1) * units)
        gate_grads.append((hidden_grad * slope[:, span]).astype(bf16))
        up_grads.append((hidden_grad * silu[:, span]).astype(bf16))
        if keep_units:
            outs[ways][:, span] = gate_grads[-1]
            outs[ways + 1][:, span] = up_grads[-1]
    for c in range(width // chunk):
        rows = slice(c * chunk, (c + 1) * chunk)
        total = dot(gate_grads[0], own[1][rows, :], (1, 1))
        total = total + dot(up_grads[0], own[2][rows, :], (1, 1))
        total = total + dot(gate_grads[1], gate[rows, :], (1, 1))
        total = total + dot(up_grads[1], up[rows, :], (1, 1))
        total = total.astype(bf16)
        for w in range(ways):
            outs[w][:, rows] = total[w * each : (w + 1) * each]


def tick_parts(sources, own, rest, keep_units):
    ways = len(sources)
    each, width = sources[0].shape
    count = ways * each
    units = own[0].shape[0]
    chunk = 512
    out_shape = [jax.ShapeDtypeStruct((each, width), bf16)] * ways
    aliases = {}
    if keep_units:
        out_shape += [jax.ShapeDtypeStruct((count, 2 * units), bf16)] * 2
    inside = pl.BlockSpec(memory_space=pltpu.VMEM)
    results = pl.pallas_call(
        lambda *refs: tick_kernel(ways, chunk, keep_units, *refs),
        out_shape=out_shape,
        in_specs=[inside] * (ways + 3 + len(rest)),
        out_specs=[inside] * len(out_shape),
        scratch_shapes=[pltpu.VMEM((count, width), bf16)],
        input_output_aliases=aliases,
        compiler_params=pltpu.CompilerParams(vmem_limit_bytes=8 * 1024 * 1024),
        cost_estimate=pl.CostEstimate(
            flops=12 * count * width * units, bytes_accessed=12 * width * units, transcendentals=0
        ),
    )(*sources, *own, *rest)
    return results[:ways], results[ways:] if keep_units else rest


def share_kernel(*refs):
    pieces, (local_ref, inputs_ref, norm_ref, out_ref) = refs[:-4], refs[-4:]
    total = pieces[0][...].astype(f32)
    for piece in pieces[1:]:
        total = total + piece[...].astype(f32)
    scale = norm_ref[...]
    exact = inputs_ref[...].astype(f32) * scale
    centre = jnp.mean(total * exact, axis=-1, keepdims=True)
    share = 0.5 * local_ref[...].astype(f32) + scale * (total - exact * centre)
    out_ref[...] = share.astype(bf16)


def advance_kernel(tick, turn_ref, straight_ref, crossed_ref, local_ref, out_ref):
    received = (straight_ref[...].astype(f32) + crossed_ref[...].astype(f32)).astype(bf16)
    out_ref[...] = jnp.where(turn_ref[0] == tick, received, local_ref[...])


def small_call(kernel, like, *operands, scalar=False):
    inside = pl.BlockSpec(memory_space=pltpu.VMEM)
    specs = [inside] * len(operands)
    if scalar:
        specs[0] = pl.BlockSpec(memory_space=pltpu.SMEM)
    return pl.pallas_call(
        kernel,
        out_shape=jax.ShapeDtypeStruct(like.shape, like.dtype),
        in_specs=specs,
        out_specs=inside,
        compiler_params=pltpu.CompilerParams(vmem_limit_bytes=4 * 1024 * 1024),
        cost_estimate=pl.CostEstimate(flops=8 * like.size, bytes_accessed=8 * like.size, transcendentals=0),
    )(*operands)


def shards(
    layer_inputs,
    cotangent,
    gate_weight,
    up_weight,
    down_weight,
    gate_momentum,
    up_momentum,
    down_momentum,
):
    segments = lax.axis_size("segment")
    tp = lax.axis_size("tp")
    depth = segments // 2
    segment = lax.axis_index("segment")
    direction = segment % 2
    position = segment // 2
    core = lax.axis_index("tp") % 2
    side = lax.axis_index("tp") // 2 % 2
    width = layer_inputs.shape[3]
    half = width // 2
    hidden_dev = gate_weight.shape[2]
    ways = tp // 4
    other_core = [(i, i ^ 1) for i in range(tp)]
    other_side = [(i, i ^ 2) for i in range(tp)]
    pair = [(i, i ^ 1) for i in range(segments)]
    mirror = [
        ((s * tp + t), ((s ^ 1) * tp + (t ^ 1))) for s in range(segments) for t in range(tp)
    ]

    def swap(block):
        return lax.ppermute(block, "tp", other_core)

    def along_y(block, distance):
        return lax.ppermute(block, "tp", [(i, (i + 4 * distance) % tp) for i in range(tp)])

    order = [1, ways - 1, *range(2, ways - 1)]

    def gathered(rows):
        out = {d: along_y(rows, d) for d in order}
        return [rows] + [out[d] for d in range(1, ways)]

    def scattered(parts):
        return [parts[0]] + [along_y(parts[d], ways - d) for d in order]

    def in_order(index, mine, theirs, axis):
        return jnp.where(
            index == 0,
            jnp.concatenate([mine, theirs], axis=axis),
            jnp.concatenate([theirs, mine], axis=axis),
        )

    trade = depth // 2
    part = jnp.where(position < trade, core, 1 - core)
    entry = lax.dynamic_index_in_dim(cotangent, direction, 0, keepdims=False)
    stacked = jnp.stack([layer_inputs[0], entry], axis=1)
    mine = lax.dynamic_index_in_dim(stacked, part, 0, keepdims=False)
    theirs = lax.dynamic_index_in_dim(stacked, 1 - part, 0, keepdims=False)
    block = in_order(core, mine, swap(theirs), 1)
    block = in_order(side, block, lax.ppermute(block, "tp", other_side), 1)
    inputs = block[0].astype(f32)
    rows_own = inputs.shape[0]
    inverse_norm = lax.rsqrt(jnp.mean(inputs * inputs, axis=-1, keepdims=True) + epsilon)
    exact = inputs * inverse_norm
    normed = exact.astype(bf16)
    local_in = block[1]

    gate_w = [gate_weight[0], swap(gate_weight[0])]
    up_w = [up_weight[0], swap(up_weight[0])]
    down_w = [down_weight[0], swap(down_weight[0])]

    first = gathered(jnp.concatenate([normed, local_in], axis=0))
    full_normed = jnp.concatenate([piece[:rows_own] for piece in first], axis=0)
    incoming = [piece[rows_own:] for piece in first]

    gate = jnp.concatenate([dot(full_normed, w, (1, 0)) for w in gate_w], axis=1)
    up = jnp.concatenate([dot(full_normed, w, (1, 0)) for w in up_w], axis=1)
    sigma = jax.nn.sigmoid(gate)
    silu = gate * sigma
    hidden = (silu * up).astype(bf16)
    slope = up * sigma * (1.0 + gate * (1.0 - sigma))

    keep = direction * half
    give = half - keep

    def features(rows, start):
        return lax.dynamic_slice_in_dim(rows, start, half, 1)

    def mirrored(rows):
        return lax.ppermute(rows, "segment", pair)

    def own(units):
        return units[:, :hidden_dev]

    def other(units):
        return units[:, hidden_dev:]

    def sent(units_own, units_other):
        return (
            units_own,
            mirrored(units_own),
            swap(units_other),
            lax.ppermute(units_other, ("segment", "tp"), mirror),
        )

    def placed(arrays, space):
        return [pltpu.with_memory_space_constraint(a, space) for a in arrays]

    own_w = placed([down_w[0], gate_w[0], up_w[0]], pltpu.VMEM)
    rest = placed([silu, slope, down_w[1], gate_w[1], up_w[1]], pltpu.VMEM)
    turn = position.astype(jnp.int32).reshape(1)
    stored = block[0]
    side_rows, side_hidden = mirrored(features(full_normed, give)), mirrored(hidden)
    for tick in range(depth):
        last = tick == depth - 1
        if tick:
            route = [(2 * tick - 2 + d, 2 * tick + d) for d in range(2)]
            turned = 1 if tick == trade else 0
            ahead = [(a * tp + t, b * tp + (t ^ turned)) for a, b in route for t in range(tp)]
            across = [(a * tp + t, b * tp + (t ^ turned ^ 2)) for a, b in route for t in range(tp)]
            straight = lax.ppermute(back, ("segment", "tp"), ahead)
            crossed = lax.ppermute(back, ("segment", "tp"), across)
            local_in = small_call(
                functools.partial(advance_kernel, tick), local_in, turn, straight, crossed, local_in, scalar=True
            )
            if tick == 2:
                local_in, side_rows, side_hidden = lax.optimization_barrier(
                    (local_in, side_rows, side_hidden)
                )
            incoming = gathered(local_in)
        parts, rest = tick_parts(incoming, own_w, rest, last)
        pieces = scattered(parts)
        back = small_call(share_kernel, local_in, *pieces, local_in, stored, inverse_norm)
    gate_grad, up_grad, full_normed, hidden, side_rows, side_hidden, incoming, _ = lax.optimization_barrier(
        (*rest, full_normed, hidden, side_rows, side_hidden, incoming, pieces[3])
    )
    full_in = jnp.concatenate(incoming, axis=0)

    quarter = rows_own // 4
    here = lax.dynamic_slice_in_dim(back, side * 2 * quarter, 2 * quarter, 0)
    there = lax.dynamic_slice_in_dim(back, (1 - side) * 2 * quarter, 2 * quarter, 0)
    arrived = lax.ppermute(there, "tp", other_side)
    total = (here.astype(f32) + arrived.astype(f32)).astype(bf16)
    mine_back = lax.dynamic_slice_in_dim(total, core * quarter, quarter, 0)
    other_back = swap(lax.dynamic_slice_in_dim(total, (1 - core) * quarter, quarter, 0))
    low = part == 0
    input_gradient = jnp.stack(
        [jnp.where(low, mine_back, other_back), jnp.where(low, other_back, mine_back)]
    )

    slopes = jnp.concatenate(
        sent(
            jnp.concatenate([own(gate_grad), own(up_grad)], axis=1),
            jnp.concatenate([other(gate_grad), other(up_grad)], axis=1),
        ),
        axis=0,
    )
    def from_both(here, there):
        return jnp.concatenate([here, swap(there)], axis=0)

    here = jnp.concatenate([features(full_in, keep), mirrored(features(full_in, give))], axis=0)
    rows_in = from_both(here, here)
    here = jnp.concatenate([features(full_normed, keep), side_rows], axis=0)
    rows_normed = from_both(here, here)
    here = jnp.concatenate([hidden, side_hidden], axis=0)
    rows_hidden = from_both(own(here), other(here))
    gate_share = dot(rows_normed, own(slopes), (0, 0))
    up_share = dot(rows_normed, other(slopes), (0, 0))
    down_share = dot(rows_hidden, rows_in, (0, 0))
    new_gate = (momentum_decay * gate_momentum[0] + gate_share)[None]
    new_up = (momentum_decay * up_momentum[0] + up_share)[None]
    new_down = (momentum_decay * down_momentum[0] + down_share)[None]
    return (input_gradient[None], new_gate, new_up, new_down)


def solution(mesh):
    return jax.shard_map(
        shards,
        mesh=mesh,
        in_specs=(
            P("segment", None, "tp", None),
            P(None, None, "tp", None),
            P("segment", None, "tp"),
            P("segment", None, "tp"),
            P("segment", "tp", None),
            P("segment", None, "tp"),
            P("segment", None, "tp"),
            P("segment", "tp", None),
        ),
        out_specs=(
            P("segment", None, "tp", None),
            P("segment", None, "tp"),
            P("segment", None, "tp"),
            P("segment", "tp", None),
        ),
        check_vma=False,
    )
```
